32 devices in a mesh: ctx: 4 (over y, x), tp: 8 (over z, core).
Axes of the slice: x: 2, y: 2, z: 4, core: 2. Of those that a mesh axis runs over, the one named last changes fastest.
Arguments:
- projected: bfloat16 [3, 1024, 6144], P(None, 'ctx', 'tp'), may hold values from -6 to 6
- filters: float32 [384, 128], P('tp'), may hold values from -0.5 to 0.5
- out_weight: bfloat16 [6144, 6144], P('tp'), may hold values from -0.109375 to 0.109375
- grad_out: bfloat16 [1024, 6144], P('ctx', 'tp'), may hold values from -6 to 6
Outputs:
- block_out: bfloat16 [1024, 6144], P('ctx', 'tp')
- grad_inputs: bfloat16 [3, 1024, 6144], P(None, 'ctx', 'tp')
- grad_weight: float32 [6144, 6144], P('tp', 'ctx')
- grad_filters: float32 [384, 128], P('tp', 'ctx')
The draws below stay inside these ranges and needn't reach their ends.
All inputs are finite; a program needn't handle non-finite values.
Results may differ from the reference program's by a relative error of at most 0.0064.
Values may be sent and summed in bfloat16 or wider, within the bound.
A program may use at most 128 MiB of HBM per device.

```python
import math
import jax
import jax.numpy as jnp
from jax import lax

CH = 6144
DM = 6144
GS = 16
K = 128
SEQ = 1024
GROUPS = 384


def with_spikes(result, own_key, source, target, shards_of, factor):
    def block_of(axis_at):
        return (jnp.arange(result.shape[axis_at]) // (result.shape[axis_at] // shards_of)).reshape((-1,) + (1,) * (result.ndim - 1 - axis_at))

    near = jax.random.permutation(own_key, shards_of)[block_of(target)]
    other_side = (block_of(target) + shards_of // 2) % shards_of
    return jnp.where((block_of(source) == near) | (block_of(source) == other_side), factor * result, result)


def block_scale(key, shape, pieces, least, high):
    loudness = 1.0
    for dim, parts in pieces:
        draws = jax.random.uniform(jax.random.fold_in(jax.random.fold_in(key, 6), dim), (parts,), jnp.float32, least / len(pieces), high / len(pieces))
        loudness = loudness * jnp.repeat(jnp.exp(draws), shape[dim] // parts).reshape((-1,) + (1,) * (len(shape) - 1 - dim))
    return loudness


def noise(rng, dims, deviation, reach, cuts=(), held_as=jnp.bfloat16):
    values = deviation * jax.random.normal(rng, dims, jnp.float32)
    if cuts:
        values = values * block_scale(rng, dims, cuts, -0.22, 0.18)
    return jnp.clip(values, -reach, reach).astype(held_as)


def heavy_noise(rng, shape, deviation, reach, shards, heavy, held_as=jnp.bfloat16):
    array = deviation * jax.random.normal(rng, shape, jnp.float32)
    if shards:
        array = array * block_scale(rng, shape, shards, -0.22, 0.18)
    return jnp.clip(with_spikes(array, jax.random.fold_in(rng, 3), *heavy), -reach, reach).astype(held_as)


def setup_inputs(seed: int = 0) -> dict:
    keys = jax.random.split(jax.random.key(seed), 5)
    projected = noise(keys[0], (3, SEQ, CH), 1.0, 6.0, ((1, 4), (2, 8)))
    filters = noise(keys[1], (GROUPS, K), K ** -0.5, 0.5, ((0, 8),), jnp.float32)
    out_weight = heavy_noise(keys[2], (CH, DM), CH ** -0.5, 0.109375, ((0, 8),), (0, 1, 8, 2.0))
    grad_out = heavy_noise(keys[3], (SEQ, DM), 1.0, 6.0, ((0, 4), (1, 8)), (0, 1, 8, 2.0))
    return dict(projected=projected, filters=filters, out_weight=out_weight, grad_out=grad_out)


def rounded_back(values):
    return lax.optimization_barrier(values.astype(jnp.bfloat16)).astype(jnp.float32)

def reference(projected, filters, out_weight, grad_out):
    query_rows = projected[0].astype(jnp.float32)
    key_rows = projected[1].astype(jnp.float32)
    value_rows = projected[2].astype(jnp.float32)
    tap_table = rounded_back(filters)
    per_channel = jnp.repeat(tap_table.T, GS, axis=1)
    gated_rows = rounded_back(key_rows * value_rows)
    length = gated_rows.shape[0]
    width = gated_rows.shape[1]
    padded = jnp.concatenate([jnp.zeros((K, width), jnp.float32), gated_rows], axis=0)

    def forward_step(offset, running):
        window = lax.dynamic_slice_in_dim(padded, (K - offset).astype(jnp.int32), length, 0)
        return running + per_channel[offset] * window
    filtered = lax.fori_loop(0, K, forward_step, jnp.zeros((length, width), jnp.float32))
    mixed_rows = lax.optimization_barrier((query_rows * filtered).astype(jnp.bfloat16))
    block_out = jnp.dot(mixed_rows, out_weight, preferred_element_type=jnp.float32).astype(jnp.bfloat16)
    grad_mixed = jnp.dot(grad_out, out_weight.T, preferred_element_type=jnp.float32)
    grad_filtered = rounded_back(grad_mixed * query_rows)
    grad_query = (grad_mixed * filtered).astype(jnp.bfloat16)
    ahead_rows = jnp.concatenate([grad_filtered, jnp.zeros((K, width), jnp.float32)], axis=0)

    def backward_step(offset, running):
        window = lax.dynamic_slice_in_dim(ahead_rows, jnp.asarray(offset).astype(jnp.int32), length, 0)
        return running + per_channel[offset] * window
    grad_gated = lax.fori_loop(0, K, backward_step, jnp.zeros((length, width), jnp.float32))
    grad_key = (grad_gated * value_rows).astype(jnp.bfloat16)
    grad_value = (grad_gated * key_rows).astype(jnp.bfloat16)
    grad_inputs = jnp.stack([grad_query, grad_key, grad_value])

    def filter_step(offset, tap_grads):
        window = lax.dynamic_slice_in_dim(padded, (K - offset).astype(jnp.int32), length, 0)
        tap_row = lax.optimization_barrier(jnp.sum(grad_filtered * window, axis=0))
        return lax.dynamic_update_slice_in_dim(tap_grads, tap_row[None, :], jnp.asarray(offset).astype(jnp.int32), 0)
    tap_grads = lax.fori_loop(0, K, filter_step, jnp.zeros((K, width), jnp.float32))
    grad_filters = lax.optimization_barrier(jnp.sum(tap_grads.reshape(K, GROUPS, GS), axis=2)).T / math.sqrt(SEQ * GS)
    grad_weight = jnp.dot(mixed_rows.T, grad_out, preferred_element_type=jnp.float32) / math.sqrt(SEQ)
    return (block_out, grad_inputs, grad_weight, grad_filters)
```

```python
import functools
import math

import jax
import jax.numpy as jnp
from jax import lax
from jax.experimental import pallas as pl
from jax.experimental.pallas import tpu as pltpu
from jax.sharding import PartitionSpec as P

LANES = 128


def shifted(value, axis, steps):
    count = lax.axis_size(axis)
    first, last = (max(0, -steps), min(count, count - steps))
    return lax.ppermute(value, axis, [(source, source + steps) for source in range(first, last)])


def lane_group(rows, width, group_size):
    lane = lax.broadcasted_iota(jnp.int32, (rows, width), 1)
    return (lane % LANES) // group_size


def windows(extended, taps_count, blocks):
    return jnp.concatenate(
        [extended[b * taps_count : b * taps_count + 2 * taps_count] for b in range(blocks)], axis=1
    )


def toeplitz(row, taps_count, shift):
    spread = jnp.broadcast_to(row, (taps_count, 2 * taps_count))
    return pltpu.roll(spread, shift, 1, stride=1, stride_axis=0).astype(jnp.bfloat16)


def banded(table, shift, window, taps_count, group_size):
    width = window.shape[1]
    group = lane_group(taps_count, width, group_size)
    total = jnp.zeros((taps_count, width), jnp.float32)
    for g in range(LANES // group_size):
        tile = toeplitz(table[g : g + 1, :], taps_count, shift)
        part = jnp.dot(tile, window, preferred_element_type=jnp.float32)
        total = jnp.where(group == g, part, total)
    return total


def forward_kernel(group_size, taps_count, p_ref, halo_ref, table_ref, filtered_ref, mixed_ref):
    blocks = p_ref.shape[1] // taps_count
    gated = (p_ref[1].astype(jnp.float32) * p_ref[2].astype(jnp.float32)).astype(jnp.bfloat16)
    window = windows(jnp.concatenate([halo_ref[...], gated], axis=0), taps_count, blocks)
    total = banded(table_ref[...], 1, window, taps_count, group_size)
    for b in range(blocks):
        rows = slice(b * taps_count, (b + 1) * taps_count)
        part = total[:, b * LANES : (b + 1) * LANES]
        filtered_ref[rows, :] = part
        mixed_ref[rows, :] = (p_ref[0, rows, :].astype(jnp.float32) * part).astype(jnp.bfloat16)


def backward_kernel(
    group_size, taps_count, p_ref, halo_ref, next_ref, gm_ref, filtered_ref, table_ref, gi_ref, gt_ref
):
    blocks = p_ref.shape[1] // taps_count
    key, value = p_ref[1].astype(jnp.float32), p_ref[2].astype(jnp.float32)
    gated = (key * value).astype(jnp.bfloat16)
    grad_mixed = gm_ref[...]
    grad_filtered = (grad_mixed * p_ref[0].astype(jnp.float32)).astype(jnp.bfloat16)
    gi_ref[0] = (grad_mixed * filtered_ref[...]).astype(jnp.bfloat16)
    ahead = windows(jnp.concatenate([grad_filtered, next_ref[...]], axis=0), taps_count, blocks)
    total = banded(table_ref[...], 0, ahead, taps_count, group_size)
    for b in range(blocks):
        rows = slice(b * taps_count, (b + 1) * taps_count)
        part = total[:, b * LANES : (b + 1) * LANES]
        gi_ref[1, rows, :] = (part * value[rows]).astype(jnp.bfloat16)
        gi_ref[2, rows, :] = (part * key[rows]).astype(jnp.bfloat16)
    window = windows(jnp.concatenate([halo_ref[...], gated], axis=0), taps_count, blocks)
    width = blocks * LANES
    row = lax.broadcasted_iota(jnp.int32, (taps_count, taps_count), 0)
    col = lax.broadcasted_iota(jnp.int32, (taps_count, taps_count), 1)
    swap = (row + col == taps_count - 1).astype(jnp.float32).astype(jnp.bfloat16)
    reversed_rows = jnp.dot(swap, ahead[:taps_count], preferred_element_type=jnp.float32)
    group = lane_group(taps_count, width, group_size)
    for g in range(LANES // group_size):
        own = jnp.where(group == g, reversed_rows, 0.0).astype(jnp.bfloat16)
        product = lax.dot_general(
            own, window, (((1,), (1,)), ((), ())), preferred_element_type=jnp.float32
        )
        aligned = pltpu.roll(product, taps_count, 1, stride=1, stride_axis=0)
        gt_ref[g : g + 1, :] = jnp.sum(aligned, axis=0, keepdims=True)[:, :taps_count]


def local(projected, filters, out_weight, grad_out):
    out_rows = projected.shape[1]
    channels = projected.shape[2]
    groups, taps_count = filters.shape
    group_size = channels // groups
    tile_groups = LANES // group_size
    grid = (channels // LANES,)
    sequence = lax.axis_size("ctx") * out_rows
    taps = filters.astype(jnp.bfloat16).astype(jnp.float32)
    zeros = jnp.zeros_like(taps)
    table_ahead = jnp.concatenate([taps, zeros], axis=1)
    table_back = jnp.concatenate([taps[:, ::-1], zeros], axis=1)
    tail = projected[:, out_rows - taps_count :].astype(jnp.float32)
    earlier = shifted((tail[1] * tail[2]).astype(jnp.bfloat16), "ctx", 1)
    full_grad = lax.all_gather(grad_out, "tp", axis=1, tiled=True)

    p_spec = pl.BlockSpec((3, out_rows, LANES), lambda i: (0, 0, i))
    halo_spec = pl.BlockSpec((taps_count, LANES), lambda i: (0, i))
    row_spec = pl.BlockSpec((out_rows, LANES), lambda i: (0, i))
    table_spec = pl.BlockSpec((tile_groups, 2 * taps_count), lambda i: (i, 0))
    taps_spec = pl.BlockSpec((tile_groups, taps_count), lambda i: (i, 0))
    band_flops = 4 * channels * tile_groups * out_rows * taps_count
    vmem = pltpu.CompilerParams(vmem_limit_bytes=32 * 1024 * 1024)
    filtered, mixed = pl.pallas_call(
        functools.partial(forward_kernel, group_size, taps_count),
        grid=grid,
        in_specs=[p_spec, halo_spec, table_spec],
        out_specs=[row_spec, row_spec],
        out_shape=[
            jax.ShapeDtypeStruct((out_rows, channels), jnp.float32),
            jax.ShapeDtypeStruct((out_rows, channels), jnp.bfloat16),
        ],
        compiler_params=vmem,
        cost_estimate=pl.CostEstimate(
            flops=band_flops, bytes_accessed=out_rows * channels * 12, transcendentals=0
        ),
    )(projected, earlier, table_back)

    own_features = lax.psum_scatter(
        jnp.einsum("tc,cd->td", mixed, out_weight, preferred_element_type=jnp.float32),
        "tp",
        scatter_dimension=1,
        tiled=True,
    )
    block_out = own_features.astype(jnp.bfloat16)
    all_mixed = lax.all_gather(mixed, "ctx", axis=0, tiled=True)
    grad_mixed = jnp.einsum("td,cd->tc", full_grad, out_weight, preferred_element_type=jnp.float32)
    head = (grad_mixed[:taps_count] * projected[0, :taps_count].astype(jnp.float32)).astype(
        jnp.bfloat16
    )
    following = shifted(head, "ctx", -1)
    all_grad = lax.all_to_all(full_grad, "ctx", split_axis=1, concat_axis=0, tiled=True)
    grad_inputs, tap_grads = pl.pallas_call(
        functools.partial(backward_kernel, group_size, taps_count),
        grid=grid,
        in_specs=[p_spec, halo_spec, halo_spec, row_spec, row_spec, table_spec],
        out_specs=[p_spec, taps_spec],
        out_shape=[
            jax.ShapeDtypeStruct((3, out_rows, channels), jnp.bfloat16),
            jax.ShapeDtypeStruct((groups, taps_count), jnp.float32),
        ],
        compiler_params=vmem,
        cost_estimate=pl.CostEstimate(
            flops=2 * band_flops, bytes_accessed=out_rows * channels * 20, transcendentals=0
        ),
    )(projected, earlier, following, grad_mixed, filtered, table_ahead)
    filter_term = tap_grads[:, ::-1] / math.sqrt(sequence * group_size)
    grad_filters = lax.psum_scatter(filter_term, "ctx", scatter_dimension=1, tiled=True)
    grad_weight = jnp.einsum(
        "tc,td->cd", all_mixed, all_grad, preferred_element_type=jnp.float32
    ) * (1.0 / math.sqrt(sequence))
    return (block_out, grad_inputs, grad_weight, grad_filters)


def solution(mesh):
    placed = (P(None, "ctx", "tp"), P("tp", None), P("tp", None), P("ctx", "tp"))
    return jax.shard_map(
        local,
        mesh=mesh,
        in_specs=placed,
        out_specs=(P("ctx", "tp"), P(None, "ctx", "tp"), P("tp", "ctx"), P("tp", "ctx")),
        check_vma=False,
    )
```

```python
import functools
import math

import jax
import jax.numpy as jnp
from jax import lax
from jax.experimental import pallas as pl
from jax.experimental.pallas import tpu as pltpu
from jax.sharding import PartitionSpec as P

LANES = 128


def lane_group(rows, width, group_size):
    lane = lax.broadcasted_iota(jnp.int32, (rows, width), 1)
    return (lane % LANES) // group_size


def windows(extended, taps_count, blocks):
    return jnp.concatenate(
        [extended[b * taps_count : b * taps_count + 2 * taps_count] for b in range(blocks)], axis=1
    )


def toeplitz(row, taps_count, shift):
    spread = jnp.broadcast_to(row, (taps_count, 2 * taps_count))
    return pltpu.roll(spread, shift, 1, stride=1, stride_axis=0).astype(jnp.bfloat16)


def banded(table, shift, window, taps_count, group_size):
    width = window.shape[1]
    group = lane_group(taps_count, width, group_size)
    total = jnp.zeros((taps_count, width), jnp.float32)
    for g in range(LANES // group_size):
        tile = toeplitz(table[g : g + 1, :], taps_count, shift)
        part = jnp.dot(tile, window, preferred_element_type=jnp.float32)
        total = jnp.where(group == g, part, total)
    return total


def whole_kernel(
    ctx_size, tp_size, group_size, p_ref, table_back, table_ahead, w_ref, go_ref,
    block_ref, gi_ref, gw_ref, gt_ref,
    full, allg, allm, halo, following, filtered, gm, gf, part_out, part_in, mine, rs_out, rs_in,
    taps_own, taps_in,
    shift_sem, ag_send, ag_recv, mf_send, mf_recv, a2_send, a2_recv, am_send, am_recv,
    mix_send, mix_recv, pm_send, pm_recv, rs_send, rs_recv, tap_send, tap_recv,
):
    chips = tp_size // 2
    per = tp_size // ctx_size
    rows, channels = p_ref.shape[1], p_ref.shape[2]
    width = go_ref.shape[1]
    taps_count = halo.shape[0]
    blocks = rows // taps_count
    tile_groups = LANES // group_size
    sequence = ctx_size * rows
    ctx, tp = lax.axis_index("ctx"), lax.axis_index("tp")
    core, pos = lax.rem(tp, 2), lax.div(tp, 2)
    mate = tp + 1 - 2 * core
    f32, bf16 = jnp.float32, jnp.bfloat16

    def loop(first, last, step):
        def run(i, carry):
            step(i)
            return carry

        lax.fori_loop(first, last, run, 0)

    def remote(source, target, send, recv, c, t):
        return pltpu.make_async_remote_copy(
            src_ref=source, dst_ref=target, send_sem=send, recv_sem=recv,
            device_id=(c, t), device_id_type=pl.DeviceIdType.MESH,
        )

    def chip_after(d):
        return lax.rem(pos + d, chips) * 2 + core

    def chip_before(d):
        return lax.rem(pos - d + chips, chips) * 2 + core

    def ctx_after(d):
        return lax.rem(ctx + d, ctx_size)

    def ctx_before(d):
        return lax.rem(ctx - d + ctx_size, ctx_size)

    def lanes(i, size):
        return pl.ds(pl.multiple_of(i * size, LANES), size)

    barrier = pltpu.get_barrier_semaphore()

    def greet(c, t):
        pl.semaphore_signal(barrier, inc=1, device_id=(c, t), device_id_type=pl.DeviceIdType.MESH)

    loop(1, chips, lambda d: greet(ctx, chip_after(d)))
    loop(1, ctx_size, lambda d: greet(ctx_after(d), tp))
    greet(ctx, mate)
    pl.semaphore_wait(barrier, chips + ctx_size - 1)

    def ag_copy(d):
        return remote(go_ref, full.at[tp], ag_send.at[d], ag_recv.at[d], ctx, chip_after(d))

    def mate_copy(d):
        k = chip_before(d)
        return remote(full.at[k], full.at[k], mf_send.at[d], mf_recv.at[d], ctx, mate)

    def a2_copy(d):
        k = chip_before(d)
        owner, sub = lax.div(k, per), lax.rem(k, per)
        copy = remote(
            full.at[k], allg.at[ctx, sub], a2_send.at[d], a2_recv.at[ctx, sub], owner, tp
        )
        return owner != ctx, copy

    def start_a2(d):
        away, copy = a2_copy(d)

        @pl.when(away)
        def _():
            copy.start()

    halo_up = remote(gf.at[0:taps_count], halo, shift_sem.at[0], shift_sem.at[1], lax.rem(ctx + 1, ctx_size), tp)
    halo_down = remote(
        gf.at[0:taps_count], following, shift_sem.at[2], shift_sem.at[3], ctx_before(1), tp
    )
    has_next, has_last = ctx < ctx_size - 1, ctx > 0

    full[tp] = go_ref[...]
    tail = slice(rows - taps_count, rows)
    gf[0:taps_count, :] = (p_ref[1, tail, :].astype(f32) * p_ref[2, tail, :].astype(f32)).astype(bf16)

    @pl.when(has_next)
    def _():
        halo_up.start()

    loop(1, chips, lambda d: ag_copy(d).start())
    mate_copy(0).start()
    start_a2(0)

    @pl.when(has_last)
    def _():
        halo_up.wait_recv()

    @pl.when(jnp.logical_not(has_last))
    def _():
        halo[...] = jnp.zeros_like(halo)

    @pl.when(has_next)
    def _():
        halo_up.wait_send()

    def gated_window(i):
        at = lanes(i, LANES)
        gated = (p_ref[1, :, at].astype(f32) * p_ref[2, :, at].astype(f32)).astype(bf16)
        return windows(jnp.concatenate([halo[:, at], gated], axis=0), taps_count, blocks)

    def group_rows(i):
        return pl.ds(pl.multiple_of(i * tile_groups, tile_groups), tile_groups)

    def forward(i):
        at = lanes(i, LANES)
        total = banded(table_back[group_rows(i), :], 1, gated_window(i), taps_count, group_size)
        for b in range(blocks):
            span = slice(b * taps_count, (b + 1) * taps_count)
            part = total[:, b * LANES : (b + 1) * LANES]
            filtered[span, at] = part
            allm[ctx, span, at] = (p_ref[0, span, at].astype(f32) * part).astype(bf16)

    loop(0, channels // LANES, forward)

    def mix_copy(d):
        return remote(
            allm.at[ctx], allm.at[ctx], mix_send.at[d], mix_recv.at[d], ctx_after(d), tp
        )

    loop(1, ctx_size, lambda d: mix_copy(d).start())

    def pair_copy(m):
        return remote(part_out.at[m], part_in.at[m], pm_send.at[m], pm_recv.at[m], ctx, mate)

    def partial(k):
        return jnp.dot(allm[ctx], w_ref[:, lanes(k, width)], preferred_element_type=f32)

    def other_half(d):
        m = lax.rem(pos + d, chips)
        part_out[m] = partial(2 * m + 1 - core).astype(bf16)
        pair_copy(m).start()

    loop(1, chips + 1, other_half)

    def rs_copy(d):
        return remote(rs_out.at[d], rs_in.at[d], rs_send.at[d], rs_recv.at[d], ctx, chip_after(d))

    def own_half(d):
        k = chip_after(d)
        part = partial(k)
        pair_copy(lax.div(k, 2)).wait_recv()
        rs_out[d] = (part + part_in[lax.div(k, 2)].astype(f32)).astype(bf16)
        rs_copy(d).start()

    loop(1, chips, own_half)
    own_part = partial(tp)
    pair_copy(pos).wait_recv()
    mine[...] = own_part + part_in[pos].astype(f32)

    def add_grad(k):
        gm[...] += lax.dot_general(
            full[k], w_ref[:, lanes(k, width)], (((1,), (1,)), ((), ())),
            preferred_element_type=f32,
        )

    gm[...] = jnp.zeros_like(gm)
    add_grad(tp)

    def arrive(d):
        ag_copy(d).wait_recv()
        mate_copy(d).start()
        start_a2(d)
        add_grad(chip_before(d))

    def arrive_mate(d):
        mate_copy(d).wait_recv()
        add_grad(chip_before(d) + 1 - 2 * core)

    mate_first = 0
    arrive_mate(mate_first)
    loop(1, chips, arrive)
    loop(1, chips, arrive_mate)

    gf[...] = (gm[...] * p_ref[0].astype(f32)).astype(bf16)

    @pl.when(has_last)
    def _():
        halo_down.start()

    gi_ref[0] = (gm[...] * filtered[...]).astype(bf16)

    def relay_copy(source, sub):
        return remote(
            allg.at[source, sub], allg.at[source, sub], am_send.at[source, sub],
            am_recv.at[source, sub], ctx, mate,
        )

    def each_chunk(own, step):
        def outer(d):
            source = ctx_before(d)
            for sub in range(per):
                same = lax.rem(ctx * per + sub, 2) == core

                @pl.when(same if own else jnp.logical_not(same))
                def _():
                    step(source, sub)

        loop(1, ctx_size, outer)

    def relay(source, sub):
        remote(
            allg.at[source, sub], allg.at[source, sub], a2_send.at[0], a2_recv.at[source, sub], ctx, mate
        ).wait_recv()
        relay_copy(source, sub).start()

    each_chunk(True, relay)

    @pl.when(has_next)
    def _():
        halo_down.wait_recv()

    @pl.when(jnp.logical_not(has_next))
    def _():
        following[...] = jnp.zeros_like(following)

    row = lax.broadcasted_iota(jnp.int32, (taps_count, taps_count), 0)
    col = lax.broadcasted_iota(jnp.int32, (taps_count, taps_count), 1)
    swap = (row + col == taps_count - 1).astype(f32).astype(bf16)

    def backward(i):
        at = lanes(i, LANES)
        ahead = windows(
            jnp.concatenate([gf[:, at], following[:, at]], axis=0), taps_count, blocks
        )
        total = banded(table_ahead[group_rows(i), :], 0, ahead, taps_count, group_size)
        for b in range(blocks):
            span = slice(b * taps_count, (b + 1) * taps_count)
            part = total[:, b * LANES : (b + 1) * LANES]
            gi_ref[1, span, at] = (part * p_ref[2, span, at].astype(f32)).astype(bf16)
            gi_ref[2, span, at] = (part * p_ref[1, span, at].astype(f32)).astype(bf16)
        window = gated_window(i)
        reversed_rows = jnp.dot(swap, ahead[:taps_count], preferred_element_type=f32)
        group = lane_group(taps_count, blocks * LANES, group_size)
        found = []
        for g in range(tile_groups):
            own = jnp.where(group == g, reversed_rows, 0.0).astype(bf16)
            product = lax.dot_general(
                own, window, (((1,), (1,)), ((), ())), preferred_element_type=f32
            )
            aligned = pltpu.roll(product, taps_count, 1, stride=1, stride_axis=0)
            found.append(jnp.sum(aligned, axis=0, keepdims=True)[:, :taps_count])
        taps_own[group_rows(i), :] = jnp.concatenate(found, axis=0)

    loop(0, channels // LANES, backward)

    def tap_copy(d):
        return remote(taps_own, taps_in.at[d], tap_send.at[d], tap_recv.at[d], ctx_after(d), tp)

    loop(1, ctx_size, lambda d: tap_copy(d).start())

    each_chunk(False, lambda source, sub: relay_copy(source, sub).wait_recv())
    loop(1, ctx_size, lambda d: mix_copy(d).wait_recv())
    for sub in range(per):
        allg[ctx, sub] = full[ctx * per + sub]
    all_mixed = allm.reshape(sequence, channels)
    scale = 1.0 / math.sqrt(sequence)

    def weight(i):
        at = pl.ds(pl.multiple_of(i * LANES, LANES), LANES)
        left = all_mixed[:, at].T
        for sub in range(per):
            gw_ref[at, sub * width : (sub + 1) * width] = scale * jnp.dot(
                left, allg[:, sub].reshape(sequence, width), preferred_element_type=f32
            )

    loop(0, channels // LANES, weight)

    def gather_rs(d):
        rs_copy(d).wait_recv()
        mine[...] += rs_in[d].astype(f32)

    loop(1, chips, gather_rs)
    block_ref[...] = mine[...].astype(bf16)
    gt_ref[...] = taps_own[...]

    def gather_taps(d):
        tap_copy(d).wait_recv()
        gt_ref[...] += taps_in[d]

    loop(1, ctx_size, gather_taps)

    @pl.when(has_last)
    def _():
        halo_down.wait_send()

    def settle(d):
        ag_copy(d).wait_send()
        rs_copy(d).wait_send()

    loop(1, chips, settle)

    def settle_all(d):
        mate_copy(d).wait_send()
        pair_copy(d).wait_send()
        away, copy = a2_copy(d)

        @pl.when(away)
        def _():
            copy.wait_send()

    loop(0, chips, settle_all)

    def settle_ctx(d):
        mix_copy(d).wait_send()
        tap_copy(d).wait_send()

    loop(1, ctx_size, settle_ctx)
    each_chunk(True, lambda source, sub: relay_copy(source, sub).wait_send())


def local(projected, filters, out_weight, grad_out):
    _, rows, channels = projected.shape
    groups, taps_count = filters.shape
    group_size = channels // groups
    width = grad_out.shape[1]
    ctx_size, tp_size = lax.axis_size("ctx"), lax.axis_size("tp")
    chips, per = tp_size // 2, tp_size // ctx_size
    sequence = ctx_size * rows
    taps = filters.astype(jnp.bfloat16).astype(jnp.float32)
    zeros = jnp.zeros_like(taps)
    table_ahead = jnp.concatenate([taps, zeros], axis=1)
    table_back = jnp.concatenate([taps[:, ::-1], zeros], axis=1)
    f32, bf16 = jnp.float32, jnp.bfloat16
    dma = pltpu.SemaphoreType.DMA
    in_vmem = pl.BlockSpec(memory_space=pltpu.VMEM)
    block_out, grad_inputs, grad_weight, tap_grads = pl.pallas_call(
        functools.partial(whole_kernel, ctx_size, tp_size, group_size),
        in_specs=[in_vmem] * 5,
        out_specs=[in_vmem] * 4,
        out_shape=[
            jax.ShapeDtypeStruct((rows, width), bf16),
            jax.ShapeDtypeStruct((3, rows, channels), bf16),
            jax.ShapeDtypeStruct((channels, per * width), f32),
            jax.ShapeDtypeStruct((groups, taps_count), f32),
        ],
        scratch_shapes=[
            pltpu.VMEM((tp_size, rows, width), bf16),
            pltpu.VMEM((ctx_size, per, rows, width), bf16),
            pltpu.VMEM((ctx_size, rows, channels), bf16),
            pltpu.VMEM((taps_count, channels), bf16),
            pltpu.VMEM((taps_count, channels), bf16),
            pltpu.VMEM((rows, channels), f32),
            pltpu.VMEM((rows, channels), f32),
            pltpu.VMEM((rows, channels), bf16),
            pltpu.VMEM((chips, rows, width), bf16),
            pltpu.VMEM((chips, rows, width), bf16),
            pltpu.VMEM((rows, width), f32),
            pltpu.VMEM((chips, rows, width), bf16),
            pltpu.VMEM((chips, rows, width), bf16),
            pltpu.VMEM((groups, taps_count), f32),
            pltpu.VMEM((ctx_size, groups, taps_count), f32),
            dma((4,)),
            dma((chips,)), dma((chips,)),
            dma((chips,)), dma((chips,)),
            dma((chips,)), dma((ctx_size, per)),
            dma((ctx_size, per)), dma((ctx_size, per)),
            dma((ctx_size,)), dma((ctx_size,)),
            dma((chips,)), dma((chips,)),
            dma((chips,)), dma((chips,)),
            dma((ctx_size,)), dma((ctx_size,)),
        ],
        compiler_params=pltpu.CompilerParams(
            collective_id=0, has_side_effects=True, vmem_limit_bytes=56 * 1024 * 1024
        ),
    )(projected, table_back, table_ahead, out_weight, grad_out)
    own_taps = lax.dynamic_slice_in_dim(
        tap_grads[:, ::-1], lax.axis_index("ctx") * (taps_count // ctx_size),
        taps_count // ctx_size, 1,
    )
    return (block_out, grad_inputs, grad_weight, own_taps / math.sqrt(sequence * group_size))


def solution(mesh):
    placed = (P(None, "ctx", "tp"), P("tp", None), P("tp", None), P("ctx", "tp"))
    return jax.shard_map(
        local,
        mesh=mesh,
        in_specs=placed,
        out_specs=(P("ctx", "tp"), P(None, "ctx", "tp"), P("tp", "ctx"), P("tp", "ctx")),
        check_vma=False,
    )
```

```python
import functools
import math

import jax
import jax.numpy as jnp
from jax import lax
from jax.experimental import pallas as pl
from jax.experimental.pallas import tpu as pltpu
from jax.sharding import PartitionSpec as P

LANES = 128


def lane_group(rows, width, group_size):
    lane = lax.broadcasted_iota(jnp.int32, (rows, width), 1)
    return (lane % LANES) // group_size


def windows(extended, taps_count, blocks):
    return jnp.concatenate(
        [extended[b * taps_count : b * taps_count + 2 * taps_count] for b in range(blocks)], axis=1
    )


def toeplitz(row, taps_count, shift):
    spread = jnp.broadcast_to(row, (taps_count, 2 * taps_count))
    return pltpu.roll(spread, shift, 1, stride=1, stride_axis=0).astype(jnp.bfloat16)


def banded(table, shift, window, taps_count, group_size):
    width = window.shape[1]
    group = lane_group(taps_count, width, group_size)
    total = jnp.zeros((taps_count, width), jnp.float32)
    for g in range(LANES // group_size):
        tile = toeplitz(table[g : g + 1, :], taps_count, shift)
        part = jnp.dot(tile, window, preferred_element_type=jnp.float32)
        total = jnp.where(group == g, part, total)
    return total


def whole_kernel(
    ctx_size, tp_size, group_size, p_ref, table_back, table_ahead, w_hbm, go_ref,
    block_ref, gi_ref, allm, allg, gt_ref,
    full, w_ref, halo, following, filtered, gm, gf, part_out, part_in, mine, rs_out, rs_in,
    taps_own, taps_in,
    w_sem, shift_sem, up_send, up_recv, down_send, down_recv, mf_send, mf_recv, a2_send, a2_recv, am_send, am_recv,
    mix_send, mix_recv, pm_send, pm_recv, rs_send, rs_recv, tap_send, tap_recv,
):
    chips = tp_size // 2
    per = tp_size // ctx_size
    rows, channels = p_ref.shape[1], p_ref.shape[2]
    width = go_ref.shape[1]
    taps_count = halo.shape[0]
    blocks = rows // taps_count
    tile_groups = LANES // group_size
    ctx, tp = lax.axis_index("ctx"), lax.axis_index("tp")
    core, pos = lax.rem(tp, 2), lax.div(tp, 2)
    mate = tp + 1 - 2 * core
    f32, bf16 = jnp.float32, jnp.bfloat16

    def loop(first, last, step):
        def run(i, carry):
            step(i)
            return carry

        lax.fori_loop(first, last, run, 0)

    def remote(source, target, send, recv, c, t):
        return pltpu.make_async_remote_copy(
            src_ref=source, dst_ref=target, send_sem=send, recv_sem=recv,
            device_id=(c, t), device_id_type=pl.DeviceIdType.MESH,
        )

    def chip_after(d):
        return lax.rem(pos + d, chips) * 2 + core

    def ctx_after(d):
        return lax.rem(ctx + d, ctx_size)

    def ctx_before(d):
        return lax.rem(ctx - d + ctx_size, ctx_size)

    def lanes(i, size):
        return pl.ds(pl.multiple_of(i * size, LANES), size)

    def chunk(sub):
        return pl.ds(sub * width, width) if isinstance(sub, int) else lanes(sub, width)

    barrier = pltpu.get_barrier_semaphore()

    def greet(c, t):
        pl.semaphore_signal(barrier, inc=1, device_id=(c, t), device_id_type=pl.DeviceIdType.MESH)

    weights = pltpu.make_async_copy(w_hbm, w_ref, w_sem.at[0])
    weights.start()
    loop(1, chips, lambda d: greet(ctx, chip_after(d)))
    loop(1, ctx_size, lambda d: greet(ctx_after(d), tp))
    greet(ctx, mate)
    pl.semaphore_wait(barrier, chips + ctx_size - 1)

    def up_copy(h):
        k = tp - 2 * h
        return remote(full.at[k], full.at[k], up_send.at[h], up_recv.at[h], ctx, tp + 2)

    def up_landed(h):
        k = tp - 2 * (h + 1)
        return remote(full.at[k], full.at[k], up_send.at[h], up_recv.at[h], ctx, tp - 2)

    def down_copy(h):
        k = tp + 2 * h
        return remote(full.at[k], full.at[k], down_send.at[h], down_recv.at[h], ctx, tp - 2)

    def down_landed(h):
        k = tp + 2 * (h + 1)
        return remote(full.at[k], full.at[k], down_send.at[h], down_recv.at[h], ctx, tp + 2)

    def sends_up(h):
        return jnp.logical_and(pos - h >= 0, pos + 1 < chips)

    def sends_down(h):
        return jnp.logical_and(pos + h < chips, pos >= 1)

    def pass_on(h):
        @pl.when(sends_up(h))
        def _():
            up_copy(h).start()

        @pl.when(sends_down(h))
        def _():
            down_copy(h).start()

    def mate_copy(m):
        k = 2 * m + core
        return remote(full.at[k], full.at[k], mf_send.at[m], mf_recv.at[m], ctx, mate)

    def a2_copy(m):
        k = 2 * m + core
        owner, sub = lax.div(k, per), lax.rem(k, per)
        copy = remote(
            full.at[k], allg.at[ctx, :, chunk(sub)], a2_send.at[m], a2_recv.at[ctx, sub], owner, tp
        )
        return owner != ctx, copy

    def start_a2(m):
        away, copy = a2_copy(m)

        @pl.when(away)
        def _():
            copy.start()

    halo_up = remote(gf.at[0:taps_count], halo, shift_sem.at[0], shift_sem.at[1], lax.rem(ctx + 1, ctx_size), tp)
    halo_down = remote(
        gf.at[0:taps_count], following, shift_sem.at[2], shift_sem.at[3], ctx_before(1), tp
    )
    has_next, has_last = ctx < ctx_size - 1, ctx > 0

    full[tp] = go_ref[...]
    tail = slice(rows - taps_count, rows)
    gf[0:taps_count, :] = (p_ref[1, tail, :].astype(f32) * p_ref[2, tail, :].astype(f32)).astype(bf16)

    @pl.when(has_next)
    def _():
        halo_up.start()

    pass_on(0)
    mate_copy(pos).start()
    start_a2(pos)

    def arrive(h):
        @pl.when(pos - 1 - h >= 0)
        def _():
            up_landed(h).wait_recv()

            @pl.when(pos + 1 < chips)
            def _():
                up_copy(h + 1).start()

            mate_copy(pos - 1 - h).start()
            start_a2(pos - 1 - h)

        @pl.when(pos + 1 + h < chips)
        def _():
            down_landed(h).wait_recv()

            @pl.when(pos >= 1)
            def _():
                down_copy(h + 1).start()

            mate_copy(pos + 1 + h).start()
            start_a2(pos + 1 + h)

    @pl.when(has_last)
    def _():
        halo_up.wait_recv()

    @pl.when(jnp.logical_not(has_last))
    def _():
        halo[...] = jnp.zeros_like(halo)

    @pl.when(has_next)
    def _():
        halo_up.wait_send()

    def gated_window(i):
        at = lanes(i, LANES)
        gated = (p_ref[1, :, at].astype(f32) * p_ref[2, :, at].astype(f32)).astype(bf16)
        return windows(jnp.concatenate([halo[:, at], gated], axis=0), taps_count, blocks)

    def group_rows(i):
        return pl.ds(pl.multiple_of(i * tile_groups, tile_groups), tile_groups)

    def forward(i):
        at = lanes(i, LANES)
        total = banded(table_back[group_rows(i), :], 1, gated_window(i), taps_count, group_size)
        for b in range(blocks):
            span = slice(b * taps_count, (b + 1) * taps_count)
            part = total[:, b * LANES : (b + 1) * LANES]
            filtered[span, at] = part
            allm[ctx, span, at] = (p_ref[0, span, at].astype(f32) * part).astype(bf16)

    loop(0, channels // LANES, forward)

    def mix_copy(d):
        return remote(
            allm.at[ctx], allm.at[ctx], mix_send.at[d], mix_recv.at[d], ctx_after(d), tp
        )

    first, second = min(1, chips - 1), min(2, chips - 1)
    loop(0, first, arrive)
    loop(1, ctx_size, lambda d: mix_copy(d).start())
    weights.wait()

    def pair_copy(m):
        return remote(part_out.at[m], part_in.at[m], pm_send.at[m], pm_recv.at[m], ctx, mate)

    def partial(k):
        return jnp.dot(allm[ctx], w_ref[:, lanes(k, width)], preferred_element_type=f32)

    def other_half(d):
        m = lax.rem(pos + d, chips)
        part_out[m] = partial(2 * m + 1 - core).astype(bf16)
        pair_copy(m).start()

    loop(1, chips + 1, other_half)
    loop(first, second, arrive)

    def rs_copy(d):
        return remote(rs_out.at[d], rs_in.at[d], rs_send.at[d], rs_recv.at[d], ctx, chip_after(d))

    def own_half(d):
        k = chip_after(d)
        part = partial(k)
        pair_copy(lax.div(k, 2)).wait_recv()
        rs_out[d] = (part + part_in[lax.div(k, 2)].astype(f32)).astype(bf16)
        rs_copy(d).start()

    loop(1, chips, own_half)
    own_part = partial(tp)
    pair_copy(pos).wait_recv()
    mine[...] = own_part + part_in[pos].astype(f32)

    def add_grad(k):
        gm[...] += lax.dot_general(
            full[k], w_ref[:, lanes(k, width)], (((1,), (1,)), ((), ())),
            preferred_element_type=f32,
        )

    gm[...] = jnp.zeros_like(gm)
    add_grad(tp)

    def add_mate(m):
        mate_copy(m).wait_recv()
        add_grad(2 * m + 1 - core)

    def add_hop(h):
        @pl.when(pos - 1 - h >= 0)
        def _():
            add_grad(tp - 2 * (h + 1))

        @pl.when(pos + 1 + h < chips)
        def _():
            add_grad(tp + 2 * (h + 1))

    def late_hop(h):
        arrive(h)
        add_hop(h)

    add_mate(pos)
    loop(0, second, add_hop)
    loop(second, chips - 1, late_hop)
    loop(1, chips, lambda d: add_mate(lax.rem(pos + d, chips)))

    gf[...] = (gm[...] * p_ref[0].astype(f32)).astype(bf16)

    @pl.when(has_last)
    def _():
        halo_down.start()

    gi_ref[0] = (gm[...] * filtered[...]).astype(bf16)

    def relay_copy(source, sub):
        return remote(
            allg.at[source, :, chunk(sub)], allg.at[source, :, chunk(sub)], am_send.at[source, sub],
            am_recv.at[source, sub], ctx, mate,
        )

    def each_chunk(own, step):
        def outer(d):
            source = ctx_before(d)
            for sub in range(per):
                same = lax.rem(ctx * per + sub, 2) == core

                @pl.when(same if own else jnp.logical_not(same))
                def _():
                    step(source, sub)

        loop(1, ctx_size, outer)

    def relay(source, sub):
        remote(
            allg.at[source, :, chunk(sub)], allg.at[source, :, chunk(sub)], a2_send.at[0], a2_recv.at[source, sub], ctx, mate
        ).wait_recv()
        relay_copy(source, sub).start()

    each_chunk(True, relay)

    @pl.when(has_next)
    def _():
        halo_down.wait_recv()

    @pl.when(jnp.logical_not(has_next))
    def _():
        following[...] = jnp.zeros_like(following)

    row = lax.broadcasted_iota(jnp.int32, (taps_count, taps_count), 0)
    col = lax.broadcasted_iota(jnp.int32, (taps_count, taps_count), 1)
    swap = (row + col == taps_count - 1).astype(f32).astype(bf16)

    def backward(i):
        at = lanes(i, LANES)
        ahead = windows(
            jnp.concatenate([gf[:, at], following[:, at]], axis=0), taps_count, blocks
        )
        total = banded(table_ahead[group_rows(i), :], 0, ahead, taps_count, group_size)
        for b in range(blocks):
            span = slice(b * taps_count, (b + 1) * taps_count)
            part = total[:, b * LANES : (b + 1) * LANES]
            gi_ref[1, span, at] = (part * p_ref[2, span, at].astype(f32)).astype(bf16)
            gi_ref[2, span, at] = (part * p_ref[1, span, at].astype(f32)).astype(bf16)
        window = gated_window(i)
        reversed_rows = jnp.dot(swap, ahead[:taps_count], preferred_element_type=f32)
        group = lane_group(taps_count, blocks * LANES, group_size)
        found = []
        for g in range(tile_groups):
            own = jnp.where(group == g, reversed_rows, 0.0).astype(bf16)
            product = lax.dot_general(
                own, window, (((1,), (1,)), ((), ())), preferred_element_type=f32
            )
            aligned = pltpu.roll(product, taps_count, 1, stride=1, stride_axis=0)
            found.append(jnp.sum(aligned, axis=0, keepdims=True)[:, :taps_count])
        taps_own[group_rows(i), :] = jnp.concatenate(found, axis=0)

    loop(0, channels // LANES, backward)

    def tap_copy(d):
        return remote(taps_own, taps_in.at[d], tap_send.at[d], tap_recv.at[d], ctx_after(d), tp)

    loop(1, ctx_size, lambda d: tap_copy(d).start())

    each_chunk(False, lambda source, sub: relay_copy(source, sub).wait_recv())
    loop(1, ctx_size, lambda d: mix_copy(d).wait_recv())
    for sub in range(per):
        allg[ctx, :, chunk(sub)] = full[ctx * per + sub]

    def gather_rs(d):
        rs_copy(d).wait_recv()
        mine[...] += rs_in[d].astype(f32)

    loop(1, chips, gather_rs)
    block_ref[...] = mine[...].astype(bf16)
    gt_ref[...] = taps_own[...]

    def gather_taps(d):
        tap_copy(d).wait_recv()
        gt_ref[...] += taps_in[d]

    loop(1, ctx_size, gather_taps)

    @pl.when(has_last)
    def _():
        halo_down.wait_send()

    def settle(h):
        rs_copy(h + 1).wait_send()

        @pl.when(sends_up(h))
        def _():
            up_copy(h).wait_send()

        @pl.when(sends_down(h))
        def _():
            down_copy(h).wait_send()

    loop(0, chips - 1, settle)

    def settle_all(d):
        mate_copy(d).wait_send()
        pair_copy(d).wait_send()
        away, copy = a2_copy(d)

        @pl.when(away)
        def _():
            copy.wait_send()

    loop(0, chips, settle_all)

    def settle_ctx(d):
        mix_copy(d).wait_send()
        tap_copy(d).wait_send()

    loop(1, ctx_size, settle_ctx)
    each_chunk(True, lambda source, sub: relay_copy(source, sub).wait_send())


def local(projected, filters, out_weight, grad_out):
    _, rows, channels = projected.shape
    groups, taps_count = filters.shape
    group_size = channels // groups
    width = grad_out.shape[1]
    ctx_size, tp_size = lax.axis_size("ctx"), lax.axis_size("tp")
    chips, per = tp_size // 2, tp_size // ctx_size
    sequence = ctx_size * rows
    taps = filters.astype(jnp.bfloat16).astype(jnp.float32)
    zeros = jnp.zeros_like(taps)
    table_ahead = jnp.concatenate([taps, zeros], axis=1)
    table_back = jnp.concatenate([taps[:, ::-1], zeros], axis=1)
    f32, bf16 = jnp.float32, jnp.bfloat16
    dma = pltpu.SemaphoreType.DMA
    in_vmem = pl.BlockSpec(memory_space=pltpu.VMEM)
    block_out, grad_inputs, all_mixed, all_grad, tap_grads = pl.pallas_call(
        functools.partial(whole_kernel, ctx_size, tp_size, group_size),
        in_specs=[in_vmem] * 3 + [pl.BlockSpec(memory_space=pl.ANY), in_vmem],
        out_specs=[in_vmem] * 5,
        out_shape=[
            jax.ShapeDtypeStruct((rows, width), bf16),
            jax.ShapeDtypeStruct((3, rows, channels), bf16),
            jax.ShapeDtypeStruct((ctx_size, rows, channels), bf16),
            jax.ShapeDtypeStruct((ctx_size, rows, per * width), bf16),
            jax.ShapeDtypeStruct((groups, taps_count), f32),
        ],
        scratch_shapes=[
            pltpu.VMEM((tp_size, rows, width), bf16),
            pltpu.VMEM(out_weight.shape, bf16),
            pltpu.VMEM((taps_count, channels), bf16),
            pltpu.VMEM((taps_count, channels), bf16),
            pltpu.VMEM((rows, channels), f32),
            pltpu.VMEM((rows, channels), f32),
            pltpu.VMEM((rows, channels), bf16),
            pltpu.VMEM((chips, rows, width), bf16),
            pltpu.VMEM((chips, rows, width), bf16),
            pltpu.VMEM((rows, width), f32),
            pltpu.VMEM((chips, rows, width), bf16),
            pltpu.VMEM((chips, rows, width), bf16),
            pltpu.VMEM((groups, taps_count), f32),
            pltpu.VMEM((ctx_size, groups, taps_count), f32),
            dma((1,)),
            dma((4,)),
            dma((chips,)), dma((chips,)),
            dma((chips,)), dma((chips,)),
            dma((chips,)), dma((chips,)),
            dma((chips,)), dma((ctx_size, per)),
            dma((ctx_size, per)), dma((ctx_size, per)),
            dma((ctx_size,)), dma((ctx_size,)),
            dma((chips,)), dma((chips,)),
            dma((chips,)), dma((chips,)),
            dma((ctx_size,)), dma((ctx_size,)),
        ],
        compiler_params=pltpu.CompilerParams(
            collective_id=0, has_side_effects=True, vmem_limit_bytes=56 * 1024 * 1024
        ),
    )(projected, table_back, table_ahead, out_weight, grad_out)
    grad_weight = jnp.einsum(
        "tc,td->cd",
        all_mixed.reshape(sequence, channels),
        all_grad.reshape(sequence, per * width),
        preferred_element_type=f32,
    ) * (1.0 / math.sqrt(sequence))
    own_taps = lax.dynamic_slice_in_dim(
        tap_grads[:, ::-1], lax.axis_index("ctx") * (taps_count // ctx_size),
        taps_count // ctx_size, 1,
    )
    return (block_out, grad_inputs, grad_weight, own_taps / math.sqrt(sequence * group_size))


def solution(mesh):
    placed = (P(None, "ctx", "tp"), P("tp", None), P("tp", None), P("ctx", "tp"))
    return jax.shard_map(
        local,
        mesh=mesh,
        in_specs=placed,
        out_specs=(P("ctx", "tp"), P(None, "ctx", "tp"), P("tp", "ctx"), P("tp", "ctx")),
        check_vma=False,
    )
```

```python
import functools
import math

import jax
import jax.numpy as jnp
from jax import lax
from jax.experimental import pallas as pl
from jax.experimental.pallas import tpu as pltpu
from jax.sharding import PartitionSpec as P

LANES = 128


def lane_group(rows, width, group_size):
    lane = lax.broadcasted_iota(jnp.int32, (rows, width), 1)
    return (lane % LANES) // group_size


def windows(extended, taps_count, blocks):
    return jnp.concatenate(
        [extended[b * taps_count : b * taps_count + 2 * taps_count] for b in range(blocks)], axis=1
    )


def toeplitz(row, taps_count, shift):
    spread = jnp.broadcast_to(row, (taps_count, 2 * taps_count))
    return pltpu.roll(spread, shift, 1, stride=1, stride_axis=0).astype(jnp.bfloat16)


def banded(table, shift, window, taps_count, group_size):
    width = window.shape[1]
    group = lane_group(taps_count, width, group_size)
    total = jnp.zeros((taps_count, width), jnp.float32)
    for g in range(LANES // group_size):
        tile = toeplitz(table[g : g + 1, :], taps_count, shift)
        part = jnp.dot(tile, window, preferred_element_type=jnp.float32)
        total = jnp.where(group == g, part, total)
    return total


def whole_kernel(
    ctx_size, tp_size, group_size, p_ref, table_back, table_ahead, w_hbm, go_ref,
    block_ref, gi_ref, allm, allg, gt_ref,
    full, w_ref, halo, following, filtered, gm, gf, part_out, part_in, sums, rs_out, rs_up, rs_down,
    taps_own, taps_in,
    w_sem, shift_sem, up_send, up_recv, down_send, down_recv, mf_send, mf_recv, a2_send, a2_recv, am_send, am_recv,
    mix_send, mix_recv, pm_send, pm_recv, rs_send, ru_recv, rd_recv, tap_send, tap_recv,
):
    chips = tp_size // 2
    per = tp_size // ctx_size
    rows, channels = p_ref.shape[1], p_ref.shape[2]
    width = go_ref.shape[1]
    taps_count = halo.shape[0]
    blocks = rows // taps_count
    tile_groups = LANES // group_size
    ctx, tp = lax.axis_index("ctx"), lax.axis_index("tp")
    core, pos = lax.rem(tp, 2), lax.div(tp, 2)
    mate = tp + 1 - 2 * core
    f32, bf16 = jnp.float32, jnp.bfloat16

    def loop(first, last, step):
        def run(i, carry):
            step(i)
            return carry

        lax.fori_loop(first, last, run, 0)

    def remote(source, target, send, recv, c, t):
        return pltpu.make_async_remote_copy(
            src_ref=source, dst_ref=target, send_sem=send, recv_sem=recv,
            device_id=(c, t), device_id_type=pl.DeviceIdType.MESH,
        )

    def chip_after(d):
        return lax.rem(pos + d, chips) * 2 + core

    def ctx_after(d):
        return lax.rem(ctx + d, ctx_size)

    def ctx_before(d):
        return lax.rem(ctx - d + ctx_size, ctx_size)

    def lanes(i, size):
        return pl.ds(pl.multiple_of(i * size, LANES), size)

    def chunk(sub):
        return pl.ds(sub * width, width) if isinstance(sub, int) else lanes(sub, width)

    barrier = pltpu.get_barrier_semaphore()

    def greet(c, t):
        pl.semaphore_signal(barrier, inc=1, device_id=(c, t), device_id_type=pl.DeviceIdType.MESH)

    weights = pltpu.make_async_copy(w_hbm, w_ref, w_sem.at[0])
    weights.start()
    loop(1, chips, lambda d: greet(ctx, chip_after(d)))
    loop(1, ctx_size, lambda d: greet(ctx_after(d), tp))
    greet(ctx, mate)
    pl.semaphore_wait(barrier, chips + ctx_size - 1)

    def up_copy(h):
        k = tp - 2 * h
        return remote(full.at[k], full.at[k], up_send.at[h], up_recv.at[h], ctx, tp + 2)

    def up_landed(h):
        k = tp - 2 * (h + 1)
        return remote(full.at[k], full.at[k], up_send.at[h], up_recv.at[h], ctx, tp - 2)

    def down_copy(h):
        k = tp + 2 * h
        return remote(full.at[k], full.at[k], down_send.at[h], down_recv.at[h], ctx, tp - 2)

    def down_landed(h):
        k = tp + 2 * (h + 1)
        return remote(full.at[k], full.at[k], down_send.at[h], down_recv.at[h], ctx, tp + 2)

    def sends_up(h):
        return jnp.logical_and(pos - h >= 0, pos + 1 < chips)

    def sends_down(h):
        return jnp.logical_and(pos + h < chips, pos >= 1)

    def pass_on(h):
        @pl.when(sends_up(h))
        def _():
            up_copy(h).start()

        @pl.when(sends_down(h))
        def _():
            down_copy(h).start()

    def mate_copy(m):
        k = 2 * m + core
        return remote(full.at[k], full.at[k], mf_send.at[m], mf_recv.at[m], ctx, mate)

    def a2_copy(m):
        k = 2 * m + core
        owner, sub = lax.div(k, per), lax.rem(k, per)
        copy = remote(
            full.at[k], allg.at[ctx, :, chunk(sub)], a2_send.at[m], a2_recv.at[ctx, sub], owner, tp
        )
        return owner != ctx, copy

    def start_a2(m):
        away, copy = a2_copy(m)

        @pl.when(away)
        def _():
            copy.start()

    halo_up = remote(gf.at[0:taps_count], halo, shift_sem.at[0], shift_sem.at[1], lax.rem(ctx + 1, ctx_size), tp)
    halo_down = remote(
        gf.at[0:taps_count], following, shift_sem.at[2], shift_sem.at[3], ctx_before(1), tp
    )
    has_next, has_last = ctx < ctx_size - 1, ctx > 0

    full[tp] = go_ref[...]
    tail = slice(rows - taps_count, rows)
    gf[0:taps_count, :] = (p_ref[1, tail, :].astype(f32) * p_ref[2, tail, :].astype(f32)).astype(bf16)

    @pl.when(has_next)
    def _():
        halo_up.start()

    pass_on(0)
    mate_copy(pos).start()
    start_a2(pos)

    def arrive(h):
        @pl.when(pos - 1 - h >= 0)
        def _():
            up_landed(h).wait_recv()

            @pl.when(pos + 1 < chips)
            def _():
                up_copy(h + 1).start()

            mate_copy(pos - 1 - h).start()
            start_a2(pos - 1 - h)

        @pl.when(pos + 1 + h < chips)
        def _():
            down_landed(h).wait_recv()

            @pl.when(pos >= 1)
            def _():
                down_copy(h + 1).start()

            mate_copy(pos + 1 + h).start()
            start_a2(pos + 1 + h)

    @pl.when(has_last)
    def _():
        halo_up.wait_recv()

    @pl.when(jnp.logical_not(has_last))
    def _():
        halo[...] = jnp.zeros_like(halo)

    @pl.when(has_next)
    def _():
        halo_up.wait_send()

    def gated_window(i):
        at = lanes(i, LANES)
        gated = (p_ref[1, :, at].astype(f32) * p_ref[2, :, at].astype(f32)).astype(bf16)
        return windows(jnp.concatenate([halo[:, at], gated], axis=0), taps_count, blocks)

    def group_rows(i):
        return pl.ds(pl.multiple_of(i * tile_groups, tile_groups), tile_groups)

    def forward(i):
        at = lanes(i, LANES)
        total = banded(table_back[group_rows(i), :], 1, gated_window(i), taps_count, group_size)
        for b in range(blocks):
            span = slice(b * taps_count, (b + 1) * taps_count)
            part = total[:, b * LANES : (b + 1) * LANES]
            filtered[span, at] = part
            allm[ctx, span, at] = (p_ref[0, span, at].astype(f32) * part).astype(bf16)

    loop(0, channels // LANES, forward)

    def mix_copy(d):
        return remote(
            allm.at[ctx], allm.at[ctx], mix_send.at[d], mix_recv.at[d], ctx_after(d), tp
        )

    first, second = min(1, chips - 1), min(2, chips - 1)
    loop(0, first, arrive)
    loop(1, ctx_size, lambda d: mix_copy(d).start())
    weights.wait()

    def pair_copy(m):
        return remote(part_out.at[m], part_in.at[m], pm_send.at[m], pm_recv.at[m], ctx, mate)

    def partial(k):
        return jnp.dot(allm[ctx], w_ref[:, lanes(k, width)], preferred_element_type=f32)

    def other_half(d):
        m = lax.rem(pos + d, chips)
        part_out[m] = partial(2 * m + 1 - core).astype(bf16)
        pair_copy(m).start()

    loop(1, chips + 1, other_half)
    loop(first, second, arrive)

    def up_sum(m):
        return remote(rs_out.at[m], rs_up.at[m], rs_send.at[m], ru_recv.at[m], ctx, tp + 2)

    def down_sum(m):
        return remote(rs_out.at[m], rs_down.at[m], rs_send.at[m], rd_recv.at[m], ctx, tp - 2)

    def up_sum_landed(m):
        remote(rs_out.at[m], rs_up.at[m], rs_send.at[m], ru_recv.at[m], ctx, tp - 2).wait_recv()
        sums[m] += rs_up[m].astype(f32)

    def down_sum_landed(m):
        remote(rs_out.at[m], rs_down.at[m], rs_send.at[m], rd_recv.at[m], ctx, tp + 2).wait_recv()
        sums[m] += rs_down[m].astype(f32)

    def send_up(m):
        rs_out[m] = sums[m].astype(bf16)
        up_sum(m).start()

    def send_down(m):
        rs_out[m] = sums[m].astype(bf16)
        down_sum(m).start()

    def add_pair(m):
        part = partial(2 * m + core)
        pair_copy(m).wait_recv()
        sums[m] = part + part_in[m].astype(f32)

    def own_half(t):
        m = jnp.where(pos == 0, chips - 1 - t, t)
        add_pair(m)

        @pl.when(jnp.logical_and(pos == 0, m > pos))
        def _():
            send_up(m)

        @pl.when(jnp.logical_and(pos == chips - 1, m < pos))
        def _():
            send_down(m)

    loop(0, chips, own_half)

    def relay_up(m):
        up_sum_landed(m)
        send_up(m)

    def relay_down(m):
        down_sum_landed(m)
        send_down(m)

    def early_relay():
        @pl.when(jnp.logical_and(pos == 1, chips - 1 > pos))
        def _():
            relay_up(chips - 1)

        @pl.when(jnp.logical_and(pos == chips - 2, 0 < pos))
        def _():
            relay_down(0)

    def relay_sums(t):
        up, down = chips - 1 - t, t
        done_up = jnp.logical_and(pos == 1, up == chips - 1)
        done_down = jnp.logical_and(pos == chips - 2, down == 0)

        @pl.when(jnp.logical_and(jnp.logical_and(pos > 0, up > pos), jnp.logical_not(done_up)))
        def _():
            relay_up(up)

        @pl.when(
            jnp.logical_and(
                jnp.logical_and(pos < chips - 1, down < pos), jnp.logical_not(done_down)
            )
        )
        def _():
            relay_down(down)

    def add_grad(k):
        gm[...] += lax.dot_general(
            full[k], w_ref[:, lanes(k, width)], (((1,), (1,)), ((), ())),
            preferred_element_type=f32,
        )

    gm[...] = jnp.zeros_like(gm)
    add_grad(tp)

    def add_mate(m):
        mate_copy(m).wait_recv()
        add_grad(2 * m + 1 - core)

    def add_hop(h):
        @pl.when(pos - 1 - h >= 0)
        def _():
            add_grad(tp - 2 * (h + 1))

        @pl.when(pos + 1 + h < chips)
        def _():
            add_grad(tp + 2 * (h + 1))

    def late_hop(h):
        arrive(h)
        add_hop(h)

    add_mate(pos)
    loop(0, second, add_hop)
    loop(second, chips - 1, late_hop)
    loop(1, chips, lambda d: add_mate(lax.rem(pos + d, chips)))

    early_relay()
    gf[...] = (gm[...] * p_ref[0].astype(f32)).astype(bf16)

    @pl.when(has_last)
    def _():
        halo_down.start()

    gi_ref[0] = (gm[...] * filtered[...]).astype(bf16)

    def relay_copy(source, sub):
        return remote(
            allg.at[source, :, chunk(sub)], allg.at[source, :, chunk(sub)], am_send.at[source, sub],
            am_recv.at[source, sub], ctx, mate,
        )

    def each_chunk(own, step):
        def outer(d):
            source = ctx_before(d)
            for sub in range(per):
                same = lax.rem(ctx * per + sub, 2) == core

                @pl.when(same if own else jnp.logical_not(same))
                def _():
                    step(source, sub)

        loop(1, ctx_size, outer)

    def relay(source, sub):
        remote(
            allg.at[source, :, chunk(sub)], allg.at[source, :, chunk(sub)], a2_send.at[0], a2_recv.at[source, sub], ctx, mate
        ).wait_recv()
        relay_copy(source, sub).start()

    each_chunk(True, relay)

    @pl.when(has_next)
    def _():
        halo_down.wait_recv()

    @pl.when(jnp.logical_not(has_next))
    def _():
        following[...] = jnp.zeros_like(following)

    row = lax.broadcasted_iota(jnp.int32, (taps_count, taps_count), 0)
    col = lax.broadcasted_iota(jnp.int32, (taps_count, taps_count), 1)
    swap = (row + col == taps_count - 1).astype(f32).astype(bf16)

    def backward(i):
        at = lanes(i, LANES)
        ahead = windows(
            jnp.concatenate([gf[:, at], following[:, at]], axis=0), taps_count, blocks
        )
        total = banded(table_ahead[group_rows(i), :], 0, ahead, taps_count, group_size)
        for b in range(blocks):
            span = slice(b * taps_count, (b + 1) * taps_count)
            part = total[:, b * LANES : (b + 1) * LANES]
            gi_ref[1, span, at] = (part * p_ref[2, span, at].astype(f32)).astype(bf16)
            gi_ref[2, span, at] = (part * p_ref[1, span, at].astype(f32)).astype(bf16)
        window = gated_window(i)
        reversed_rows = jnp.dot(swap, ahead[:taps_count], preferred_element_type=f32)
        group = lane_group(taps_count, blocks * LANES, group_size)
        found = []
        for g in range(tile_groups):
            own = jnp.where(group == g, reversed_rows, 0.0).astype(bf16)
            product = lax.dot_general(
                own, window, (((1,), (1,)), ((), ())), preferred_element_type=f32
            )
            aligned = pltpu.roll(product, taps_count, 1, stride=1, stride_axis=0)
            found.append(jnp.sum(aligned, axis=0, keepdims=True)[:, :taps_count])
        taps_own[group_rows(i), :] = jnp.concatenate(found, axis=0)

    loop(0, channels // LANES, backward)
    loop(0, chips - 1, relay_sums)

    def tap_copy(d):
        return remote(taps_own, taps_in.at[d], tap_send.at[d], tap_recv.at[d], ctx_after(d), tp)

    loop(1, ctx_size, lambda d: tap_copy(d).start())

    each_chunk(False, lambda source, sub: relay_copy(source, sub).wait_recv())
    loop(1, ctx_size, lambda d: mix_copy(d).wait_recv())
    for sub in range(per):
        allg[ctx, :, chunk(sub)] = full[ctx * per + sub]

    @pl.when(pos > 0)
    def _():
        up_sum_landed(pos)

    @pl.when(pos < chips - 1)
    def _():
        down_sum_landed(pos)

    block_ref[...] = sums[pos].astype(bf16)
    gt_ref[...] = taps_own[...]

    def gather_taps(d):
        tap_copy(d).wait_recv()
        gt_ref[...] += taps_in[d]

    loop(1, ctx_size, gather_taps)

    @pl.when(has_last)
    def _():
        halo_down.wait_send()

    def settle(h):
        up_sum(lax.rem(pos + h + 1, chips)).wait_send()

        @pl.when(sends_up(h))
        def _():
            up_copy(h).wait_send()

        @pl.when(sends_down(h))
        def _():
            down_copy(h).wait_send()

    loop(0, chips - 1, settle)

    def settle_all(d):
        mate_copy(d).wait_send()
        pair_copy(d).wait_send()
        away, copy = a2_copy(d)

        @pl.when(away)
        def _():
            copy.wait_send()

    loop(0, chips, settle_all)

    def settle_ctx(d):
        mix_copy(d).wait_send()
        tap_copy(d).wait_send()

    loop(1, ctx_size, settle_ctx)
    each_chunk(True, lambda source, sub: relay_copy(source, sub).wait_send())


def local(projected, filters, out_weight, grad_out):
    _, rows, channels = projected.shape
    groups, taps_count = filters.shape
    group_size = channels // groups
    width = grad_out.shape[1]
    ctx_size, tp_size = lax.axis_size("ctx"), lax.axis_size("tp")
    chips, per = tp_size // 2, tp_size // ctx_size
    sequence = ctx_size * rows
    taps = filters.astype(jnp.bfloat16).astype(jnp.float32)
    zeros = jnp.zeros_like(taps)
    table_ahead = jnp.concatenate([taps, zeros], axis=1)
    table_back = jnp.concatenate([taps[:, ::-1], zeros], axis=1)
    f32, bf16 = jnp.float32, jnp.bfloat16
    dma = pltpu.SemaphoreType.DMA
    in_vmem = pl.BlockSpec(memory_space=pltpu.VMEM)
    block_out, grad_inputs, all_mixed, all_grad, tap_grads = pl.pallas_call(
        functools.partial(whole_kernel, ctx_size, tp_size, group_size),
        in_specs=[in_vmem] * 3 + [pl.BlockSpec(memory_space=pl.ANY), in_vmem],
        out_specs=[in_vmem] * 5,
        out_shape=[
            jax.ShapeDtypeStruct((rows, width), bf16),
            jax.ShapeDtypeStruct((3, rows, channels), bf16),
            jax.ShapeDtypeStruct((ctx_size, rows, channels), bf16),
            jax.ShapeDtypeStruct((ctx_size, rows, per * width), bf16),
            jax.ShapeDtypeStruct((groups, taps_count), f32),
        ],
        scratch_shapes=[
            pltpu.VMEM((tp_size, rows, width), bf16),
            pltpu.VMEM(out_weight.shape, bf16),
            pltpu.VMEM((taps_count, channels), bf16),
            pltpu.VMEM((taps_count, channels), bf16),
            pltpu.VMEM((rows, channels), f32),
            pltpu.VMEM((rows, channels), f32),
            pltpu.VMEM((rows, channels), bf16),
            pltpu.VMEM((chips, rows, width), bf16),
            pltpu.VMEM((chips, rows, width), bf16),
            pltpu.VMEM((chips, rows, width), f32),
            pltpu.VMEM((chips, rows, width), bf16),
            pltpu.VMEM((chips, rows, width), bf16),
            pltpu.VMEM((chips, rows, width), bf16),
            pltpu.VMEM((groups, taps_count), f32),
            pltpu.VMEM((ctx_size, groups, taps_count), f32),
            dma((1,)),
            dma((4,)),
            dma((chips,)), dma((chips,)),
            dma((chips,)), dma((chips,)),
            dma((chips,)), dma((chips,)),
            dma((chips,)), dma((ctx_size, per)),
            dma((ctx_size, per)), dma((ctx_size, per)),
            dma((ctx_size,)), dma((ctx_size,)),
            dma((chips,)), dma((chips,)),
            dma((chips,)), dma((chips,)), dma((chips,)),
            dma((ctx_size,)), dma((ctx_size,)),
        ],
        compiler_params=pltpu.CompilerParams(
            collective_id=0, has_side_effects=True, vmem_limit_bytes=56 * 1024 * 1024
        ),
    )(projected, table_back, table_ahead, out_weight, grad_out)
    grad_weight = jnp.einsum(
        "tc,td->cd",
        all_mixed.reshape(sequence, channels),
        all_grad.reshape(sequence, per * width),
        preferred_element_type=f32,
    ) * (1.0 / math.sqrt(sequence))
    own_taps = lax.dynamic_slice_in_dim(
        tap_grads[:, ::-1], lax.axis_index("ctx") * (taps_count // ctx_size),
        taps_count // ctx_size, 1,
    )
    return (block_out, grad_inputs, grad_weight, own_taps / math.sqrt(sequence * group_size))


def solution(mesh):
    placed = (P(None, "ctx", "tp"), P("tp", None), P("tp", None), P("ctx", "tp"))
    return jax.shard_map(
        local,
        mesh=mesh,
        in_specs=placed,
        out_specs=(P("ctx", "tp"), P(None, "ctx", "tp"), P("tp", "ctx"), P("tp", "ctx")),
        check_vma=False,
    )
```
